512 devices in a mesh: section: 16 (over x, y_hi, core), tp: 32 (over y_lo, z).
Axes of the slice: x: 4, y: 8 (y_hi: 2, y_lo: 4; y = y_hi * 4 + y_lo), z: 8, core: 2. Of those that a mesh axis runs over, the one named last changes fastest.
Arguments:
- inputs: bfloat16 [2, 2, 64, 4096], P(None, None, None, 'tp'), may hold values from -6 to 6
- weights: bfloat16 [8, 4096, 4096], P(None, 'section', 'tp'), may hold values from -0.09375 to 0.09375
- targets: bfloat16 [2, 2, 64, 4096], P(None, None, None, 'tp'), may hold values from -6 to 6
Outputs:
- grads: bfloat16 [8, 4096, 4096], P(None, 'section', 'tp')
The draws below stay inside these ranges and needn't reach their ends.
All inputs are finite; a program needn't handle non-finite values.
Results may differ from the reference program's by a relative error of at most 0.015.
Values may be sent and summed in bfloat16 or wider, within the bound.
No kernel may reach another device: no remote copies, remote signals or barrier semaphores. Data moves between devices by JAX's collectives and lax.ppermute only.
A program may use at most 64 MiB of HBM per device.

```python
import jax
import jax.numpy as jnp
from jax import lax

D = 4096
M = 64
MICRO = 2
SECTIONS = 8


def level_of(key, extent, pieces, smallest, top_value):
    def one(dim, parts):
        heights = jax.random.uniform(jax.random.fold_in(jax.random.fold_in(key, 6), dim), (parts,), jnp.float32, smallest / len(pieces), top_value / len(pieces))
        return jnp.repeat(jnp.exp(heights), extent[dim] // parts).reshape((-1,) + (1,) * (len(extent) - dim - 1))

    loudness = one(*pieces[0])
    for cut in pieces[1:]:
        loudness = loudness * one(*cut)
    return loudness


def normal_values(own_key, shape, spread, limit, split=(), held_as=jnp.bfloat16):
    gain = level_of(own_key, shape, split, -0.22, 0.18) if split else 1.0
    values = jax.random.normal(own_key, shape, jnp.float32) * spread * gain
    return jnp.minimum(jnp.maximum(values, -limit), limit).astype(held_as)


def setup_inputs(seed: int = 0) -> dict:
    streams_of = jax.random.split(jax.random.key(seed), 4)
    return {
        "inputs": normal_values(streams_of[0], (2, MICRO, M, D), 1.0, 6.0, ((3, 32),)),
        "weights": normal_values(streams_of[1], (SECTIONS, D, D), D ** -0.5, 0.09375, ((1, 16), (2, 32))),
        "targets": normal_values(streams_of[2], (2, MICRO, M, D), 1.0, 6.0, ((3, 32),)),
    }


EPSILON = 1e-05

def silu_slope(activation):
    sigmoid = jax.nn.sigmoid(activation)
    return sigmoid * (1.0 + activation * (1.0 - sigmoid))

def reference(inputs, weights, targets):
    features = weights.shape[1]
    accumulated = [jnp.zeros((features, features), jnp.float32) for layer_index in range(SECTIONS)]
    for direction in range(2):
        for micro_index in range(MICRO):
            hidden_state = inputs[direction, micro_index]
            stored = []
            for layer_index in range(SECTIONS):
                product = jnp.dot(hidden_state, weights[layer_index], preferred_element_type=jnp.float32)
                inverse_rms = lax.rsqrt(lax.optimization_barrier(jnp.mean(jnp.square(hidden_state.astype(jnp.float32)), axis=1)) + EPSILON)
                activation = inverse_rms[:, None] * product
                stored.append((hidden_state, product, inverse_rms, activation))
                hidden_state = (hidden_state.astype(jnp.float32) + jax.nn.silu(activation)).astype(jnp.bfloat16)
            cotangent = (hidden_state.astype(jnp.float32) - targets[direction, micro_index].astype(jnp.float32)) / M
            for layer_index in reversed(range(SECTIONS)):
                section_input, product, inverse_rms, activation = stored[layer_index]
                scaled_grad = (inverse_rms[:, None] * cotangent * silu_slope(activation)).astype(jnp.bfloat16)
                piece = jnp.dot(section_input.T, scaled_grad, preferred_element_type=jnp.float32)
                accumulated[layer_index] = accumulated[layer_index] + lax.optimization_barrier(piece.astype(jnp.bfloat16)).astype(jnp.float32)
                row_total = lax.optimization_barrier(jnp.sum(scaled_grad.astype(jnp.float32) * product, axis=1))
                returned = cotangent + jnp.dot(scaled_grad, weights[layer_index].T, preferred_element_type=jnp.float32)
                returned = returned - (inverse_rms * inverse_rms / features * row_total)[:, None] * section_input.astype(jnp.float32)
                cotangent = lax.optimization_barrier(returned.astype(jnp.bfloat16)).astype(jnp.float32)
    return jnp.stack([member.astype(jnp.bfloat16) for member in accumulated])
```

```python
import jax
import jax.numpy as jnp
from jax import lax
from jax.sharding import PartitionSpec as P

EPSILON = 1e-05
F32 = jnp.float32
BF16 = jnp.bfloat16


def silu_slope(activation):
    sigmoid = jax.nn.sigmoid(activation)
    return sigmoid * (1.0 + activation * (1.0 - sigmoid))


def spread(block, copies):
    return lax.optimization_barrier(jnp.broadcast_to(block[None], (copies,) + block.shape))


def exchanged(blocks, axis):
    return lax.all_to_all(blocks, axis, split_axis=0, concat_axis=0, tiled=True)


def on_device(inputs, weights, targets):
    groups = lax.axis_size("section")
    members = lax.axis_size("tp")
    group = lax.axis_index("section")
    sections, row_count, columns = weights.shape
    features = columns * members
    micro_tokens = inputs.shape[2]
    all_tokens = inputs.shape[0] * inputs.shape[1] * micro_tokens
    tokens = all_tokens // groups
    own_x = lax.dynamic_slice_in_dim(inputs.reshape(all_tokens, columns), group * tokens, tokens, 0)
    own_target = lax.dynamic_slice_in_dim(
        targets.reshape(all_tokens, columns), group * tokens, tokens, 0
    )
    matrices = lax.all_gather(weights, "section", axis=1, tiled=True)

    kept = []
    x = own_x
    for s in range(sections):
        blocks = exchanged(spread(x, members), "tp")
        full = blocks.transpose(1, 0, 2).reshape(tokens, features)
        product = jnp.dot(full, matrices[s], preferred_element_type=F32)
        squares = jnp.sum(jnp.square(full.astype(F32)), axis=1)
        inverse_rms = lax.rsqrt(squares / features + EPSILON)
        activation = inverse_rms[:, None] * product
        kept.append((blocks, full, product, inverse_rms, activation))
        x = (x.astype(F32) + jax.nn.silu(activation)).astype(BF16)

    cotangent = (x.astype(F32) - own_target.astype(F32)) / micro_tokens
    grads_h = [None] * sections
    for s in reversed(range(sections)):
        blocks, full, product, inverse_rms, activation = kept[s]
        h = (inverse_rms[:, None] * cotangent * silu_slope(activation)).astype(BF16)
        grads_h[s] = h
        if s == 0:
            break
        share = jnp.sum(h.astype(F32) * product, axis=1)
        back = lax.dot_general(h, matrices[s], (((1,), (1,)), ((), ())), preferred_element_type=F32)
        back = back - (inverse_rms * inverse_rms / features * share)[:, None] * full.astype(F32)
        parts = back.astype(BF16).reshape(tokens, members, columns).transpose(1, 0, 2)
        got = exchanged(parts, "tp")
        cotangent = (cotangent + jnp.sum(got.astype(F32), axis=0)).astype(BF16).astype(F32)

    outgoing = []
    for s in range(sections):
        rows = kept[s][0].reshape(groups, members // groups, tokens, columns)
        outgoing.append(rows)
        outgoing.append(jnp.broadcast_to(grads_h[s][None, None], (groups, 1, tokens, columns)))
    per = members // groups + 1
    arrived = exchanged(jnp.concatenate(outgoing, axis=1), "section")
    arrived = arrived.reshape(groups, sections, per, tokens, columns).transpose(1, 2, 0, 3, 4)
    arrived = arrived.reshape(sections, per, all_tokens, columns)
    result = []
    for s in range(sections):
        left = arrived[s, : per - 1]
        right = arrived[s, per - 1]
        result.append(
            lax.dot_general(left, right, (((1,), (0,)), ((), ())), preferred_element_type=F32)
            .astype(BF16)
            .reshape(row_count, columns)
        )
    return jnp.stack(result)


def solution(mesh):
    placed = (P(None, None, None, "tp"), P(None, "section", "tp"), P(None, None, None, "tp"))
    return jax.shard_map(
        on_device, mesh=mesh, in_specs=placed, out_specs=P(None, "section", "tp"), check_vma=False
    )
```

```python
import functools

import jax
import jax.numpy as jnp
from jax import lax
from jax.experimental import pallas as pl
from jax.experimental.pallas import tpu as pltpu
from jax.sharding import Mesh, PartitionSpec as P

EPSILON = 1e-05
F32 = jnp.float32
BF16 = jnp.bfloat16
TP = "tp"
SECTION = ("x", "far", "core")
EARLY = 3
CHUNKS = 4
RIDERS = (0, 2, 2, 2, 2, 0, 0)


def spread(block, copies):
    return lax.optimization_barrier(jnp.broadcast_to(block[None], (copies,) + block.shape))


def exchanged(blocks, axis):
    return lax.all_to_all(blocks, axis, split_axis=0, concat_axis=0, tiled=True)


def swapped(block, axis):
    return lax.ppermute(block, axis, [(0, 1), (1, 0)])


def in_order(own, other, axis, at):
    first = lax.axis_index(axis) == 0
    return jnp.stack([jnp.where(first, own, other), jnp.where(first, other, own)], axis=at)


def fetched_matrices(weights, own_x, members):
    sections, row_count, columns = weights.shape
    first = weights[:EARLY]
    crossed = swapped(first, "far")
    blocks = exchanged(spread(own_x, members), TP)
    crossed, blocks, last = lax.optimization_barrier((crossed, blocks, weights[EARLY:]))
    crossed_last = swapped(last, "far")
    pair = in_order(first, crossed, "far", 1).reshape(EARLY, 2 * row_count, columns)
    mine = exchanged(spread(pair, lax.axis_size("x")), "x")
    crossed_last, mine = lax.optimization_barrier((crossed_last, mine))
    pair = in_order(last, crossed_last, "far", 1).reshape(-1, 2 * row_count, columns)
    late = lax.all_gather(pair, ("x", "core"), axis=1, tiled=True)
    both = in_order(mine, swapped(mine, "core"), "core", 1)
    early = both.transpose(2, 0, 1, 3, 4).reshape(EARLY, -1, columns)
    late = pltpu.with_memory_space_constraint(late, pltpu.HBM)
    early = pltpu.with_memory_space_constraint(early, pltpu.HBM)
    matrices = [(early, s) for s in range(EARLY)]
    matrices += [(late, s) for s in range(sections - EARLY)]
    return matrices, blocks


def block_order(far, cores, across, per):
    return [
        ((x * far + f) * cores + c) * per + b
        for x in range(across)
        for c in range(cores)
        for f in range(far)
        for b in range(per)
    ]


def fetches(layer, matrices, held, arrived):
    rows = held.shape[0] // CHUNKS
    copies = []
    for n in range(CHUNKS):
        part = pl.ds(n * rows, rows)
        copy = pltpu.make_async_copy(matrices.at[layer, part], held.at[part], arrived.at[n])
        copy.start()
        copies.append(copy)
    return copies


def forward_kernel(order, layer, got, x, matrices, *rest):
    *sent, x_new, slope, scaled, held, arrived = rest
    copies = fetches(layer, matrices, held, arrived)
    features, columns = held.shape
    squares = jnp.zeros(x.shape, F32)
    for m in range(len(order)):
        squares += jnp.square(got[m].astype(F32))
    mean = jnp.sum(squares, axis=1, keepdims=True) / features
    inverse_rms = lax.rsqrt(mean + EPSILON)
    product = jnp.zeros(x.shape, F32)
    rows, count = features // CHUNKS, len(order) // CHUNKS
    for n in range(CHUNKS):
        segment = jnp.concatenate([got[m] for m in order[n * count : (n + 1) * count]], axis=1)
        copies[n].wait()
        product += jnp.dot(segment, held[pl.ds(n * rows, rows), :], preferred_element_type=F32)
    activation = inverse_rms * product
    sigmoid = jax.nn.sigmoid(activation)
    result = (x[...].astype(F32) + activation * sigmoid).astype(BF16)
    x_new[...] = result
    for target in sent:
        target[...] = jnp.broadcast_to(result[None], target.shape)
    slope[...] = inverse_rms * sigmoid * (1.0 + activation * (1.0 - sigmoid))
    scaled[...] = product * (inverse_rms * inverse_rms / features)


def backward_kernel(order, layer, riding, *refs):
    if riding:
        riders, *refs = refs
    received, cotangent, slope, scaled, blocks, matrices, *rest = refs
    parts, h_out, cot_out, held, arrived = rest
    copies = fetches(layer, matrices, held, arrived)
    if riding:
        for n in range(riding):
            parts[:, 1 + n] = jnp.broadcast_to(riders[n][None], (len(order),) + riders.shape[1:])
    cot = cotangent[...]
    if len(received.shape) == 3:
        total = cot
        for m in range(len(order)):
            total += received[m].astype(F32)
        cot = total.astype(BF16).astype(F32)
    cot_out[...] = cot
    h = (slope[...] * cot).astype(BF16)
    h_out[...] = h
    share = jnp.sum(h.astype(F32) * scaled[...], axis=1, keepdims=True)
    features, columns = held.shape
    rows, count = features // CHUNKS, len(order) // CHUNKS
    for n in range(CHUNKS):
        copies[n].wait()
        back = lax.dot_general(
            h,
            held[pl.ds(n * rows, rows), :],
            (((1,), (1,)), ((), ())),
            preferred_element_type=F32,
        )
        for k in range(count):
            m = order[n * count + k]
            mine = back[:, k * columns : (k + 1) * columns] - share * blocks[m].astype(F32)
            if riding:
                parts[m, 0] = mine.astype(BF16)
            else:
                parts[m] = mine.astype(BF16)


def local_call(kernel, outs, features, columns, specs):
    vmem = pl.BlockSpec(memory_space=pltpu.VMEM)
    hbm = pl.BlockSpec(memory_space=pltpu.HBM)
    return pl.pallas_call(
        kernel,
        out_shape=[pltpu.VMEM(shape, dtype) for shape, dtype in outs],
        in_specs=[vmem if spec else hbm for spec in specs],
        out_specs=[vmem] * len(outs),
        scratch_shapes=[
            pltpu.VMEM((features, columns), BF16),
            pltpu.SemaphoreType.DMA((CHUNKS,)),
        ],
        compiler_params=pltpu.CompilerParams(vmem_limit_bytes=16 * 2**20),
    )


def forward_layer(order, layer, got, x, matrices, sending):
    members, tokens, columns = got.shape
    outs = [(got.shape, BF16)] if sending else []
    outs += [(x.shape, BF16), (x.shape, F32), (x.shape, F32)]
    kernel = functools.partial(forward_kernel, order, layer)
    call = local_call(kernel, outs, members * columns, columns, (True, True, False))
    return call(got, x, matrices)


def backward_layer(order, layer, received, cotangent, slope, scaled, blocks, matrices, riders):
    members, tokens, columns = blocks.shape
    riding = 0 if riders is None else riders.shape[0]
    shape = (members, 1 + riding, tokens, columns) if riding else blocks.shape
    outs = [(shape, BF16), (cotangent.shape, BF16), (cotangent.shape, F32)]
    kernel = functools.partial(backward_kernel, order, layer, riding)
    blocks = pltpu.with_memory_space_constraint(blocks, pltpu.VMEM)
    given = ([riders] if riding else []) + [received, cotangent, slope, scaled, blocks, matrices]
    specs = [True] * (len(given) - 1) + [False]
    return local_call(kernel, outs, members * columns, columns, specs)(*given)


def moved_rows(x_stack, groups, members):
    per = members // groups
    pairs = [
        (g * members + per * r + b, r * members + per * g + b)
        for g in range(groups)
        for r in range(groups)
        for b in range(per)
    ]
    return lax.ppermute(x_stack, SECTION + (TP,), pairs)


def on_device(inputs, weights, targets):
    groups = lax.axis_size(SECTION)
    members = lax.axis_size(TP)
    group = lax.axis_index(SECTION)
    across, cores = lax.axis_size("x"), lax.axis_size("core")
    sections, row_count, columns = weights.shape
    micro_tokens = inputs.shape[2]
    all_tokens = inputs.shape[0] * inputs.shape[1] * micro_tokens
    tokens = all_tokens // groups
    per = members // groups
    own_x = lax.dynamic_slice_in_dim(inputs.reshape(all_tokens, columns), group * tokens, tokens, 0)
    own_target = lax.dynamic_slice_in_dim(
        targets.reshape(all_tokens, columns), group * tokens, tokens, 0
    )
    matrices, blocks = fetched_matrices(weights, own_x, members)

    order = block_order(2, cores, across, per)
    kept = []
    xs = [own_x]
    for s in range(sections):
        held, at = matrices[s]
        *sent, x, slope, scaled = forward_layer(order, at, blocks, xs[-1], held, s < sections - 1)
        kept.append((blocks, slope, scaled))
        if sent:
            xs.append(x)
            blocks = exchanged(sent[0], TP)

    riders = moved_rows(jnp.stack(xs), groups, members)
    all_rows = []
    cotangent = (x.astype(F32) - own_target.astype(F32)) / micro_tokens
    grads_h = [None] * sections
    received = x
    for s in range(sections - 1, 0, -1):
        blocks, slope, scaled = kept[s]
        held, at = matrices[s]
        count = RIDERS[sections - 1 - s]
        taken = riders[len(all_rows) : len(all_rows) + count] if count else None
        parts, grads_h[s], cotangent = backward_layer(
            order, at, received, cotangent, slope, scaled, blocks, held, taken
        )
        received = exchanged(parts, TP)
        if count:
            all_rows.extend(received[:, 1 + n] for n in range(count))
            received = received[:, 0]
    cotangent = (cotangent + jnp.sum(received.astype(F32), axis=0)).astype(BF16).astype(F32)
    grads_h[0] = (kept[0][1] * cotangent).astype(BF16)

    h_all = exchanged(spread(jnp.stack(grads_h), groups), SECTION)
    result = []
    for s in range(sections):
        left = all_rows[s].reshape(groups, per, tokens, columns)
        result.append(
            lax.dot_general(
                left, h_all[:, s], (((0, 2), (0, 1)), ((), ())), preferred_element_type=F32
            )
            .astype(BF16)
            .reshape(row_count, columns)
        )
    return jnp.stack(result)


def solution(mesh):
    devices = mesh.devices.reshape(4, 2, 2, mesh.shape[TP])
    finer = Mesh(devices, SECTION + (TP,))
    matrix = P(None, SECTION, TP)
    placed = (P(None, None, None, TP), matrix, P(None, None, None, TP))
    return jax.shard_map(
        on_device, mesh=finer, in_specs=placed, out_specs=matrix, check_vma=False
    )
```

```python
import functools

import jax
import jax.numpy as jnp
from jax import lax
from jax.experimental import pallas as pl
from jax.experimental.pallas import tpu as pltpu
from jax.sharding import Mesh, PartitionSpec as P

EPSILON = 1e-05
F32 = jnp.float32
BF16 = jnp.bfloat16
TP = "tp"
SECTION = ("x", "far", "core")
ACROSS, FAR, CORES = 4, 2, 2
EARLY = 3


def spread(block, copies):
    return lax.optimization_barrier(jnp.broadcast_to(block[None], (copies,) + block.shape))


def exchanged(blocks, axis):
    return lax.all_to_all(blocks, axis, split_axis=0, concat_axis=0, tiled=True)


def swapped(block, axis):
    return lax.ppermute(block, axis, [(0, 1), (1, 0)])


def fetched_matrices(weights, own_x, members):
    sections, row_count, columns = weights.shape
    first = weights[:EARLY]
    crossed = swapped(first, "far")
    blocks = exchanged(spread(own_x, members), TP)
    crossed, blocks, last = lax.optimization_barrier((crossed, blocks, weights[EARLY:]))
    crossed_last = swapped(last, "far")
    pair = jnp.stack([first, crossed], axis=1).reshape(-1, columns)
    mine = exchanged(spread(pair, ACROSS), "x")
    crossed_last, mine = lax.optimization_barrier((crossed_last, mine))
    pair = jnp.stack([last, crossed_last], axis=1).reshape(-1, 2 * row_count, columns)
    late = lax.all_gather(pair, ("x", "core"), axis=1, tiled=True)
    return blocks, (close(mine), close(swapped(mine, "core"))), (close(late),)


def block_order(early, per):
    far, core = lax.axis_index("far"), lax.axis_index("core")
    order = []
    for x in range(ACROSS):
        for k in range(CORES):
            owner = lax.rem(core + k, CORES) if early else k
            for q in range(FAR):
                section = (x * FAR + lax.rem(far + q, FAR)) * CORES + owner
                order += [per * section + b for b in range(per)]
    return order


def rows_of(layer, sources, n, rows):
    if len(sources) == 2:
        return sources[n % CORES][n // CORES, pl.ds(layer * rows, rows)]
    return sources[0][layer - EARLY, pl.ds(n * rows, rows)]


def forward_kernel(layer, per, count_in, got, x, *refs):
    sources, (*sent, x_new, slope, scaled) = refs[:count_in], refs[count_in:]
    members, tokens, columns = got.shape
    features = members * columns
    squares = jnp.zeros(x.shape, F32)
    for m in range(members):
        squares += jnp.square(got[m].astype(F32))
    mean = jnp.sum(squares, axis=1, keepdims=True) / features
    inverse_rms = lax.rsqrt(mean + EPSILON)
    order = block_order(layer < EARLY, per)
    count = ACROSS * CORES
    rows, blocks = features // count, members // count
    product = jnp.zeros(x.shape, F32)
    for n in range(count):
        segment = jnp.concatenate([got[m] for m in order[n * blocks : (n + 1) * blocks]], axis=1)
        product += jnp.dot(
            segment, rows_of(layer, sources, n, rows), preferred_element_type=F32
        )
    activation = inverse_rms * product
    sigmoid = jax.nn.sigmoid(activation)
    result = (x[...].astype(F32) + activation * sigmoid).astype(BF16)
    x_new[...] = result
    for target in sent:
        target[...] = jnp.broadcast_to(result[None], target.shape)
    slope[...] = inverse_rms * sigmoid * (1.0 + activation * (1.0 - sigmoid))
    scaled[...] = product * (inverse_rms * inverse_rms / features)


def backward_kernel(layer, per, count_in, received, cotangent, slope, scaled, got, *refs):
    sources, (parts, h_out, cot_out) = refs[:count_in], refs[count_in:]
    members, tokens, columns = got.shape
    cot = cotangent[...]
    if len(received.shape) == 3:
        total = cot
        for m in range(members):
            total += received[m].astype(F32)
        cot = total.astype(BF16).astype(F32)
    cot_out[...] = cot
    h = (slope[...] * cot).astype(BF16)
    h_out[...] = h
    share = jnp.sum(h.astype(F32) * scaled[...], axis=1, keepdims=True)
    order = block_order(layer < EARLY, per)
    count = ACROSS * CORES
    rows, blocks = members * columns // count, members // count
    for n in range(count):
        back = lax.dot_general(
            h,
            rows_of(layer, sources, n, rows),
            (((1,), (1,)), ((), ())),
            preferred_element_type=F32,
        )
        for k in range(blocks):
            m = order[n * blocks + k]
            mine = back[:, k * columns : (k + 1) * columns] - share * got[m].astype(F32)
            parts[m] = mine.astype(BF16)


def last_kernel(per, received, cotangent, slope, *refs):
    *others, packed = refs
    sections = (len(others) + 1) // 2
    gots, later = others[:sections], others[sections:]
    tokens = slope.shape[0]
    total = cotangent[...]
    for m in range(received.shape[0]):
        total += received[m].astype(F32)
    h = (slope[...] * total.astype(BF16).astype(F32)).astype(BF16)
    for s, block in enumerate([h] + [other[...] for other in later]):
        for g in range(packed.shape[0]):
            at = s * (per + 1) * tokens
            for b in range(per):
                packed[g, pl.ds(at + b * tokens, tokens)] = gots[s][per * g + b]
            packed[g, pl.ds(at + per * tokens, tokens)] = block


def grads_kernel(per, tokens, arrived, out):
    groups, _, columns = arrived.shape
    for s in range(out.shape[0]):
        at = s * (per + 1) * tokens
        gathered = [
            jnp.concatenate(
                [arrived[g, pl.ds(at + b * tokens, tokens)] for g in range(groups)], axis=0
            )
            for b in range(per + 1)
        ]
        for b in range(per):
            total = lax.dot_general(
                gathered[b], gathered[per], (((0,), (0,)), ((), ())), preferred_element_type=F32
            )
            out[s, pl.ds(b * columns, columns)] = total.astype(BF16)


def local_call(kernel, outs, *inputs):
    vmem = pl.BlockSpec(memory_space=pltpu.VMEM)
    call = pl.pallas_call(
        kernel,
        out_shape=[jax.ShapeDtypeStruct(shape, dtype) for shape, dtype in outs],
        in_specs=[vmem] * len(inputs),
        out_specs=[vmem] * len(outs),
        compiler_params=pltpu.CompilerParams(vmem_limit_bytes=32 * 2**20),
    )
    return call(*inputs)


def close(array):
    return pltpu.with_memory_space_constraint(array, pltpu.VMEM)


def on_device(inputs, weights, targets):
    groups = lax.axis_size(SECTION)
    members = lax.axis_size(TP)
    group = lax.axis_index(SECTION)
    sections, row_count, columns = weights.shape
    micro_tokens = inputs.shape[2]
    all_tokens = inputs.shape[0] * inputs.shape[1] * micro_tokens
    tokens = all_tokens // groups
    per = members // groups
    block = (tokens, columns)
    own_x = lax.dynamic_slice_in_dim(inputs.reshape(all_tokens, columns), group * tokens, tokens, 0)
    own_target = lax.dynamic_slice_in_dim(
        targets.reshape(all_tokens, columns), group * tokens, tokens, 0
    )
    blocks, early, late = fetched_matrices(weights, own_x, members)

    kept = []
    x = own_x
    for s in range(sections):
        sources = early if s < EARLY else late
        outs = [((members,) + block, BF16)] if s < sections - 1 else []
        outs += [(block, BF16), (block, F32), (block, F32)]
        kernel = functools.partial(forward_kernel, s, per, len(sources))
        *sent, x, slope, scaled = local_call(kernel, outs, blocks, x, *sources)
        kept.append((blocks, slope, scaled))
        if sent:
            blocks = exchanged(sent[0], TP)

    cotangent = (x.astype(F32) - own_target.astype(F32)) / micro_tokens
    grads_h = []
    received = x
    for s in range(sections - 1, 0, -1):
        sources = early if s < EARLY else late
        blocks, slope, scaled = kept[s]
        outs = [((members,) + block, BF16), (block, BF16), (block, F32)]
        kernel = functools.partial(backward_kernel, s, per, len(sources))
        parts, h, cotangent = local_call(
            kernel, outs, received, cotangent, slope, scaled, blocks, *sources
        )
        grads_h.insert(0, h)
        received = exchanged(parts, TP)
    (packed,) = local_call(
        functools.partial(last_kernel, per),
        [((groups, sections * (per + 1) * tokens, columns), BF16)],
        received,
        cotangent,
        kept[0][1],
        *[entry[0] for entry in kept],
        *grads_h,
    )
    (result,) = local_call(
        functools.partial(grads_kernel, per, tokens),
        [(weights.shape, BF16)],
        exchanged(packed, SECTION),
    )
    return result


def solution(mesh):
    devices = mesh.devices.reshape(ACROSS, FAR, CORES, mesh.shape[TP])
    finer = Mesh(devices, SECTION + (TP,))
    matrix = P(None, SECTION, TP)
    placed = (P(None, None, None, TP), matrix, P(None, None, None, TP))
    return jax.shard_map(
        on_device, mesh=finer, in_specs=placed, out_specs=matrix, check_vma=False
    )
```

```python
import functools

import jax
import jax.numpy as jnp
from jax import lax
from jax.experimental import pallas as pl
from jax.experimental.pallas import tpu as pltpu
from jax.sharding import Mesh, PartitionSpec as P

EPSILON = 1e-05
F32 = jnp.float32
BF16 = jnp.bfloat16
TP = "tp"
SECTION = ("x", "far", "core")
ACROSS, FAR, CORES = 4, 2, 2
EARLY = 3


def spread(block, copies):
    return lax.optimization_barrier(jnp.broadcast_to(block[None], (copies,) + block.shape))


def exchanged(blocks, axis):
    return lax.all_to_all(blocks, axis, split_axis=0, concat_axis=0, tiled=True)


def swapped(block, axis):
    return lax.ppermute(block, axis, [(0, 1), (1, 0)])


def gathered(shard, crossed):
    pair = jnp.concatenate([shard, crossed], axis=1)
    return pair, functools.partial(lax.all_gather, axis_name=("x", "core"), axis=1, tiled=True)


def fetched_matrices(weights, own_x, members):
    first = weights[:EARLY]
    crossed = swapped(first, "far")
    pair, gather = gathered(first, crossed)
    pair, own_x, last = lax.optimization_barrier((pair, own_x, weights[EARLY:]))
    early = gather(pair)
    crossed_last = swapped(last, "far")
    blocks = exchanged(spread(own_x, members), TP)
    pair, gather = gathered(last, crossed_last)
    pair, blocks = lax.optimization_barrier((pair, blocks))
    late = gather(pair)
    return blocks, close(early), close(late)


def block_order(per):
    far = lax.axis_index("far")
    order = []
    for x in range(ACROSS):
        for core in range(CORES):
            for q in range(FAR):
                section = (x * FAR + lax.rem(far + q, FAR)) * CORES + core
                order += [per * section + b for b in range(per)]
    return order


def forward_kernel(layer, per, got, x, matrices, *outs):
    *sent, x_new, slope, scaled = outs
    members, tokens, columns = got.shape
    features = members * columns
    squares = jnp.zeros(x.shape, F32)
    for m in range(members):
        squares += jnp.square(got[m].astype(F32))
    mean = jnp.sum(squares, axis=1, keepdims=True) / features
    inverse_rms = lax.rsqrt(mean + EPSILON)
    order = block_order(per)
    count = ACROSS * CORES
    rows, blocks = features // count, members // count
    product = jnp.zeros(x.shape, F32)
    for n in range(count):
        segment = jnp.concatenate([got[m] for m in order[n * blocks : (n + 1) * blocks]], axis=1)
        product += jnp.dot(
            segment, matrices[layer, pl.ds(n * rows, rows)], preferred_element_type=F32
        )
    activation = inverse_rms * product
    sigmoid = jax.nn.sigmoid(activation)
    result = (x[...].astype(F32) + activation * sigmoid).astype(BF16)
    x_new[...] = result
    for target in sent:
        target[...] = jnp.broadcast_to(result[None], target.shape)
    slope[...] = inverse_rms * sigmoid * (1.0 + activation * (1.0 - sigmoid))
    scaled[...] = product * (inverse_rms * inverse_rms / features)


def backward_kernel(layer, per, micro_tokens, received, cotangent, slope, scaled, got, matrices, *outs):
    parts, h_out, cot_out = outs
    members, tokens, columns = got.shape
    if len(received.shape) == 2:
        cot = (received[...].astype(F32) - cotangent[...].astype(F32)) / micro_tokens
    else:
        total = cotangent[...]
        for m in range(members):
            total += received[m].astype(F32)
        cot = total.astype(BF16).astype(F32)
    cot_out[...] = cot
    h = (slope[...] * cot).astype(BF16)
    h_out[...] = h
    share = jnp.sum(h.astype(F32) * scaled[...], axis=1, keepdims=True)
    order = block_order(per)
    count = ACROSS * CORES
    rows, blocks = members * columns // count, members // count
    for n in range(count):
        back = lax.dot_general(
            h,
            matrices[layer, pl.ds(n * rows, rows)],
            (((1,), (1,)), ((), ())),
            preferred_element_type=F32,
        )
        for k in range(blocks):
            m = order[n * blocks + k]
            mine = back[:, k * columns : (k + 1) * columns] - share * got[m].astype(F32)
            parts[m] = mine.astype(BF16)


def last_kernel(per, received, cotangent, slope, *refs):
    *others, packed = refs
    sections = (len(others) + 1) // 2
    gots, later = others[:sections], others[sections:]
    tokens = slope.shape[0]
    total = cotangent[...]
    for m in range(received.shape[0]):
        total += received[m].astype(F32)
    h = (slope[...] * total.astype(BF16).astype(F32)).astype(BF16)
    for s, block in enumerate([h] + [other[...] for other in later]):
        for g in range(packed.shape[0]):
            at = s * (per + 1) * tokens
            for b in range(per):
                packed[g, pl.ds(at + b * tokens, tokens)] = gots[s][per * g + b]
            packed[g, pl.ds(at + per * tokens, tokens)] = block


def grads_kernel(per, tokens, arrived, out):
    groups, _, columns = arrived.shape
    for s in range(out.shape[0]):
        at = s * (per + 1) * tokens
        gathered = [
            jnp.concatenate(
                [arrived[g, pl.ds(at + b * tokens, tokens)] for g in range(groups)], axis=0
            )
            for b in range(per + 1)
        ]
        for b in range(per):
            total = lax.dot_general(
                gathered[b], gathered[per], (((0,), (0,)), ((), ())), preferred_element_type=F32
            )
            out[s, pl.ds(b * columns, columns)] = total.astype(BF16)


def local_call(kernel, outs, *inputs):
    vmem = pl.BlockSpec(memory_space=pltpu.VMEM)
    call = pl.pallas_call(
        kernel,
        out_shape=[jax.ShapeDtypeStruct(shape, dtype) for shape, dtype in outs],
        in_specs=[vmem] * len(inputs),
        out_specs=[vmem] * len(outs),
        compiler_params=pltpu.CompilerParams(vmem_limit_bytes=32 * 2**20),
    )
    return call(*inputs)


def close(array):
    return pltpu.with_memory_space_constraint(array, pltpu.VMEM)


def on_device(inputs, weights, targets):
    groups = lax.axis_size(SECTION)
    members = lax.axis_size(TP)
    group = lax.axis_index(SECTION)
    sections, row_count, columns = weights.shape
    micro_tokens = inputs.shape[2]
    all_tokens = inputs.shape[0] * inputs.shape[1] * micro_tokens
    tokens = all_tokens // groups
    per = members // groups
    block = (tokens, columns)
    own_x = lax.dynamic_slice_in_dim(inputs.reshape(all_tokens, columns), group * tokens, tokens, 0)
    own_target = lax.dynamic_slice_in_dim(
        targets.reshape(all_tokens, columns), group * tokens, tokens, 0
    )
    blocks, early, late = fetched_matrices(weights, own_x, members)

    kept = []
    x = own_x
    for s in range(sections):
        matrices, at = (early, s) if s < EARLY else (late, s - EARLY)
        outs = [((members,) + block, BF16)] if s < sections - 1 else []
        outs += [(block, BF16), (block, F32), (block, F32)]
        kernel = functools.partial(forward_kernel, at, per)
        *sent, x, slope, scaled = local_call(kernel, outs, blocks, x, matrices)
        kept.append((blocks, slope, scaled))
        if sent:
            blocks = exchanged(sent[0], TP)

    grads_h = []
    received, cotangent = x, own_target
    for s in range(sections - 1, 0, -1):
        matrices, at = (early, s) if s < EARLY else (late, s - EARLY)
        blocks, slope, scaled = kept[s]
        outs = [((members,) + block, BF16), (block, BF16), (block, F32)]
        kernel = functools.partial(backward_kernel, at, per, micro_tokens)
        parts, h, cotangent = local_call(
            kernel, outs, received, cotangent, slope, scaled, blocks, matrices
        )
        grads_h.insert(0, h)
        received = exchanged(parts, TP)
    (packed,) = local_call(
        functools.partial(last_kernel, per),
        [((groups, sections * (per + 1) * tokens, columns), BF16)],
        received,
        cotangent,
        kept[0][1],
        *[entry[0] for entry in kept],
        *grads_h,
    )
    (result,) = local_call(
        functools.partial(grads_kernel, per, tokens),
        [(weights.shape, BF16)],
        exchanged(packed, SECTION),
    )
    return result


def solution(mesh):
    devices = mesh.devices.reshape(ACROSS, FAR, CORES, mesh.shape[TP])
    finer = Mesh(devices, SECTION + (TP,))
    matrix = P(None, SECTION, TP)
    placed = (P(None, None, None, TP), matrix, P(None, None, None, TP))
    return jax.shard_map(
        on_device, mesh=finer, in_specs=placed, out_specs=matrix, check_vma=False
    )
```

```python
import functools

import jax
import jax.numpy as jnp
from jax import lax
from jax.experimental import pallas as pl
from jax.experimental.pallas import tpu as pltpu
from jax.sharding import Mesh, PartitionSpec as P

EPSILON = 1e-05
F32 = jnp.float32
BF16 = jnp.bfloat16
TP = "tp"
SECTION = ("x", "far", "core")
ACROSS, FAR, CORES = 4, 2, 2
EARLY = 3
FETCHING = (0, EARLY)


def spread(block, copies):
    return lax.optimization_barrier(jnp.broadcast_to(block[None], (copies,) + block.shape))


def exchanged(blocks, axis):
    return lax.all_to_all(blocks, axis, split_axis=0, concat_axis=0, tiled=True)


def swapped(block, axis):
    return lax.ppermute(block, axis, [(0, 1), (1, 0)])


def gathered(shard, crossed):
    pair = jnp.concatenate([shard, crossed], axis=1)
    return pair, functools.partial(lax.all_gather, axis_name=("x", "core"), axis=1, tiled=True)


def fetched_matrices(weights, own_x, members):
    first = weights[:EARLY]
    crossed = swapped(first, "far")
    pair, gather = gathered(first, crossed)
    pair, own_x, last = lax.optimization_barrier((pair, own_x, weights[EARLY:]))
    early = gather(pair)
    crossed_last = swapped(last, "far")
    blocks = exchanged(spread(own_x, members), TP)
    pair, gather = gathered(last, crossed_last)
    pair, blocks = lax.optimization_barrier((pair, blocks))
    late = gather(pair)
    return blocks, early, late


def block_order(per):
    far = lax.axis_index("far")
    order = []
    for x in range(ACROSS):
        for core in range(CORES):
            for q in range(FAR):
                section = (x * FAR + lax.rem(far + q, FAR)) * CORES + core
                order += [per * section + b for b in range(per)]
    return order


def forward_kernel(layer, per, fetching, got, x, matrices, *refs):
    if fetching:
        *refs, held, arrived = refs
    *sent, x_new, slope, scaled = refs
    members, tokens, columns = got.shape
    features = members * columns
    order = block_order(per)
    count = ACROSS * CORES
    rows, blocks = features // count, members // count
    copies = []
    for n in range(count if fetching else 0):
        part = pl.ds(n * rows, rows)
        copies.append(
            pltpu.make_async_copy(matrices.at[layer, part], held.at[part], arrived.at[n])
        )
        copies[n].start()
    squares = jnp.zeros(x.shape, F32)
    for m in range(members):
        squares += jnp.square(got[m].astype(F32))
    mean = jnp.sum(squares, axis=1, keepdims=True) / features
    inverse_rms = lax.rsqrt(mean + EPSILON)
    product = jnp.zeros(x.shape, F32)
    for n in range(count):
        segment = jnp.concatenate([got[m] for m in order[n * blocks : (n + 1) * blocks]], axis=1)
        part = pl.ds(n * rows, rows)
        if fetching:
            copies[n].wait()
        matrix = held[part] if fetching else matrices[layer, part]
        product += jnp.dot(segment, matrix, preferred_element_type=F32)
    activation = inverse_rms * product
    sigmoid = jax.nn.sigmoid(activation)
    result = (x[...].astype(F32) + activation * sigmoid).astype(BF16)
    x_new[...] = result
    for target in sent:
        target[...] = jnp.broadcast_to(result[None], target.shape)
    slope[...] = inverse_rms * sigmoid * (1.0 + activation * (1.0 - sigmoid))
    scaled[...] = product * (inverse_rms * inverse_rms / features)


def backward_kernel(layer, per, micro_tokens, received, cotangent, slope, scaled, got, matrices, *outs):
    parts, h_out, cot_out = outs
    members, tokens, columns = got.shape
    if len(received.shape) == 2:
        cot = (received[...].astype(F32) - cotangent[...].astype(F32)) / micro_tokens
    else:
        total = cotangent[...]
        for m in range(members):
            total += received[m].astype(F32)
        cot = total.astype(BF16).astype(F32)
    cot_out[...] = cot
    h = (slope[...] * cot).astype(BF16)
    h_out[...] = h
    share = jnp.sum(h.astype(F32) * scaled[...], axis=1, keepdims=True)
    order = block_order(per)
    count = ACROSS * CORES
    rows, blocks = members * columns // count, members // count
    for n in range(count):
        back = lax.dot_general(
            h,
            matrices[layer, pl.ds(n * rows, rows)],
            (((1,), (1,)), ((), ())),
            preferred_element_type=F32,
        )
        for k in range(blocks):
            m = order[n * blocks + k]
            mine = back[:, k * columns : (k + 1) * columns] - share * got[m].astype(F32)
            parts[m] = mine.astype(BF16)


def last_kernel(per, received, cotangent, slope, *refs):
    *others, packed = refs
    sections = (len(others) + 1) // 2
    gots, later = others[:sections], others[sections:]
    tokens = slope.shape[0]
    total = cotangent[...]
    for m in range(received.shape[0]):
        total += received[m].astype(F32)
    h = (slope[...] * total.astype(BF16).astype(F32)).astype(BF16)
    for s, block in enumerate([h] + [other[...] for other in later]):
        for g in range(packed.shape[0]):
            at = s * (per + 1) * tokens
            for b in range(per):
                packed[g, pl.ds(at + b * tokens, tokens)] = gots[s][per * g + b]
            packed[g, pl.ds(at + per * tokens, tokens)] = block


def grads_kernel(per, tokens, arrived, out):
    groups, _, columns = arrived.shape
    for s in range(out.shape[0]):
        at = s * (per + 1) * tokens
        gathered = [
            jnp.concatenate(
                [arrived[g, pl.ds(at + b * tokens, tokens)] for g in range(groups)], axis=0
            )
            for b in range(per + 1)
        ]
        for b in range(per):
            total = lax.dot_general(
                gathered[b], gathered[per], (((0,), (0,)), ((), ())), preferred_element_type=F32
            )
            out[s, pl.ds(b * columns, columns)] = total.astype(BF16)


def local_call(kernel, outs, *inputs, fetching=False, scratch=()):
    vmem = pl.BlockSpec(memory_space=pltpu.VMEM)
    there = pl.BlockSpec(memory_space=pl.ANY)
    call = pl.pallas_call(
        kernel,
        out_shape=[jax.ShapeDtypeStruct(shape, dtype) for shape, dtype in outs],
        in_specs=[vmem] * (len(inputs) - fetching) + [there] * fetching,
        out_specs=[vmem] * len(outs),
        scratch_shapes=list(scratch),
        compiler_params=pltpu.CompilerParams(vmem_limit_bytes=32 * 2**20),
    )
    return call(*inputs)


def close(array):
    return pltpu.with_memory_space_constraint(array, pltpu.VMEM)


def on_device(inputs, weights, targets):
    groups = lax.axis_size(SECTION)
    members = lax.axis_size(TP)
    group = lax.axis_index(SECTION)
    sections, row_count, columns = weights.shape
    micro_tokens = inputs.shape[2]
    all_tokens = inputs.shape[0] * inputs.shape[1] * micro_tokens
    tokens = all_tokens // groups
    per = members // groups
    block = (tokens, columns)
    own_x = lax.dynamic_slice_in_dim(inputs.reshape(all_tokens, columns), group * tokens, tokens, 0)
    own_target = lax.dynamic_slice_in_dim(
        targets.reshape(all_tokens, columns), group * tokens, tokens, 0
    )
    own_x, own_target = lax.optimization_barrier((own_x, own_target))
    blocks, early, late = fetched_matrices(weights, own_x, members)

    scratch = [
        pltpu.VMEM((members * columns, columns), BF16),
        pltpu.SemaphoreType.DMA((ACROSS * CORES,)),
    ]
    early_there, late_there = [
        pltpu.with_memory_space_constraint(array, pltpu.HBM) for array in (early, late)
    ]
    early, late = close(early), close(late)
    kept = []
    x = own_x
    for s in range(sections):
        fetching = s in FETCHING
        if s < EARLY:
            matrices, at = early_there if fetching else early, s
        else:
            matrices, at = late_there if fetching else late, s - EARLY
        outs = [((members,) + block, BF16)] if s < sections - 1 else []
        outs += [(block, BF16), (block, F32), (block, F32)]
        kernel = functools.partial(forward_kernel, at, per, fetching)
        given = (kernel, outs, blocks, x, matrices)
        *sent, x, slope, scaled = local_call(
            *given, fetching=fetching, scratch=scratch if fetching else ()
        )
        kept.append((blocks, slope, scaled))
        if sent:
            blocks = exchanged(sent[0], TP)

    grads_h = []
    received, cotangent = x, own_target
    for s in range(sections - 1, 0, -1):
        matrices, at = (early, s) if s < EARLY else (late, s - EARLY)
        blocks, slope, scaled = kept[s]
        outs = [((members,) + block, BF16), (block, BF16), (block, F32)]
        kernel = functools.partial(backward_kernel, at, per, micro_tokens)
        parts, h, cotangent = local_call(
            kernel, outs, received, cotangent, slope, scaled, blocks, matrices
        )
        grads_h.insert(0, h)
        received = exchanged(parts, TP)
    (packed,) = local_call(
        functools.partial(last_kernel, per),
        [((groups, sections * (per + 1) * tokens, columns), BF16)],
        received,
        cotangent,
        kept[0][1],
        *[entry[0] for entry in kept],
        *grads_h,
    )
    (result,) = local_call(
        functools.partial(grads_kernel, per, tokens),
        [(weights.shape, BF16)],
        exchanged(packed, SECTION),
    )
    return result


def solution(mesh):
    devices = mesh.devices.reshape(ACROSS, FAR, CORES, mesh.shape[TP])
    finer = Mesh(devices, SECTION + (TP,))
    matrix = P(None, SECTION, TP)
    placed = (P(None, None, None, TP), matrix, P(None, None, None, TP))
    return jax.shard_map(
        on_device, mesh=finer, in_specs=placed, out_specs=matrix, check_vma=False
    )
```

```python
import functools

import jax
import jax.numpy as jnp
from jax import lax
from jax.experimental import pallas as pl
from jax.experimental.pallas import tpu as pltpu
from jax.sharding import Mesh, PartitionSpec as P

EPSILON = 1e-05
F32 = jnp.float32
BF16 = jnp.bfloat16
TP = "tp"
SECTION = ("x", "far", "core")
ACROSS, FAR, CORES = 4, 2, 2
EARLY = 3
FETCHING = (0, 2, EARLY)


def spread(block, copies):
    return lax.optimization_barrier(jnp.broadcast_to(block[None], (copies,) + block.shape))


def exchanged(blocks, axis):
    return lax.all_to_all(blocks, axis, split_axis=0, concat_axis=0, tiled=True)


def swapped(block, axis):
    return lax.ppermute(block, axis, [(0, 1), (1, 0)])


def gathered(shard, crossed):
    pair = jnp.concatenate([shard, crossed], axis=1)
    return pair, functools.partial(lax.all_gather, axis_name=("x", "core"), axis=1, tiled=True)


def fetched_matrices(weights, own_x, members):
    first = weights[:EARLY]
    crossed = swapped(first, "far")
    pair, gather = gathered(first, crossed)
    pair, own_x, last = lax.optimization_barrier((pair, own_x, weights[EARLY:]))
    early = gather(pair)
    crossed_last = swapped(last, "far")
    blocks = exchanged(spread(own_x, members), TP)
    pair, gather = gathered(last, crossed_last)
    pair, blocks = lax.optimization_barrier((pair, blocks))
    late = gather(pair)
    return blocks, early, late


def block_order(per):
    far = lax.axis_index("far")
    order = []
    for x in range(ACROSS):
        for core in range(CORES):
            for q in range(FAR):
                section = (x * FAR + lax.rem(far + q, FAR)) * CORES + core
                order += [per * section + b for b in range(per)]
    return order


def forward_kernel(layer, per, fetching, got, x, matrices, *refs):
    if fetching:
        *refs, held, arrived = refs
    *sent, x_new, factors = refs
    members, tokens, columns = got.shape
    features = members * columns
    order = block_order(per)
    count = ACROSS * CORES
    rows, blocks = features // count, members // count
    copies = []
    for n in range(count if fetching else 0):
        part = pl.ds(n * rows, rows)
        copies.append(
            pltpu.make_async_copy(matrices.at[layer, part], held.at[part], arrived.at[n])
        )
        copies[n].start()
    squares = jnp.zeros(x.shape, F32)
    for m in range(members):
        squares += jnp.square(got[m].astype(F32))
    mean = jnp.sum(squares, axis=1, keepdims=True) / features
    inverse_rms = lax.rsqrt(mean + EPSILON)
    product = jnp.zeros(x.shape, F32)
    for n in range(count):
        segment = jnp.concatenate([got[m] for m in order[n * blocks : (n + 1) * blocks]], axis=1)
        part = pl.ds(n * rows, rows)
        if fetching:
            copies[n].wait()
        matrix = held[part] if fetching else matrices[layer, part]
        product += jnp.dot(segment, matrix, preferred_element_type=F32)
    activation = inverse_rms * product
    sigmoid = jax.nn.sigmoid(activation)
    result = (x[...].astype(F32) + activation * sigmoid).astype(BF16)
    x_new[...] = result
    for target in sent:
        target[...] = jnp.broadcast_to(result[None], target.shape)
    factors[0] = inverse_rms * sigmoid * (1.0 + activation * (1.0 - sigmoid))
    factors[1] = product * (inverse_rms * inverse_rms / features)


def backward_kernel(layer, per, micro_tokens, received, cotangent, factors, got, matrices, *outs):
    parts, h_out, cot_out = outs
    members, tokens, columns = got.shape
    if len(received.shape) == 2:
        cot = (received[...].astype(F32) - cotangent[...].astype(F32)) / micro_tokens
    else:
        total = cotangent[...]
        for m in range(members):
            total += received[m].astype(F32)
        cot = total.astype(BF16).astype(F32)
    cot_out[...] = cot
    h = (factors[0] * cot).astype(BF16)
    h_out[...] = h
    share = jnp.sum(h.astype(F32) * factors[1], axis=1, keepdims=True)
    order = block_order(per)
    count = ACROSS * CORES
    rows, blocks = members * columns // count, members // count
    for n in range(count):
        back = lax.dot_general(
            h,
            matrices[layer, pl.ds(n * rows, rows)],
            (((1,), (1,)), ((), ())),
            preferred_element_type=F32,
        )
        for k in range(blocks):
            m = order[n * blocks + k]
            mine = back[:, k * columns : (k + 1) * columns] - share * got[m].astype(F32)
            parts[m] = mine.astype(BF16)


def last_kernel(per, received, cotangent, factors, *refs):
    *others, packed = refs
    sections = (len(others) + 1) // 2
    gots, later = others[:sections], others[sections:]
    tokens = cotangent.shape[0]
    total = cotangent[...]
    for m in range(received.shape[0]):
        total += received[m].astype(F32)
    h = (factors[0] * total.astype(BF16).astype(F32)).astype(BF16)
    for s, block in enumerate([h] + [other[...] for other in later]):
        for g in range(packed.shape[0]):
            at = s * (per + 1) * tokens
            for b in range(per):
                packed[g, pl.ds(at + b * tokens, tokens)] = gots[s][per * g + b]
            packed[g, pl.ds(at + per * tokens, tokens)] = block


def grads_kernel(per, tokens, arrived, out):
    groups, _, columns = arrived.shape
    for s in range(out.shape[0]):
        at = s * (per + 1) * tokens
        gathered = [
            jnp.concatenate(
                [arrived[g, pl.ds(at + b * tokens, tokens)] for g in range(groups)], axis=0
            )
            for b in range(per + 1)
        ]
        for b in range(per):
            total = lax.dot_general(
                gathered[b], gathered[per], (((0,), (0,)), ((), ())), preferred_element_type=F32
            )
            out[s, pl.ds(b * columns, columns)] = total.astype(BF16)


def local_call(kernel, outs, *inputs, fetching=False, scratch=()):
    vmem = pl.BlockSpec(memory_space=pltpu.VMEM)
    there = pl.BlockSpec(memory_space=pl.ANY)
    call = pl.pallas_call(
        kernel,
        out_shape=[jax.ShapeDtypeStruct(shape, dtype) for shape, dtype in outs],
        in_specs=[vmem] * (len(inputs) - fetching) + [there] * fetching,
        out_specs=[vmem] * len(outs),
        scratch_shapes=list(scratch),
        compiler_params=pltpu.CompilerParams(vmem_limit_bytes=32 * 2**20),
    )
    return call(*inputs)


def close(array):
    return pltpu.with_memory_space_constraint(array, pltpu.VMEM)


def on_device(inputs, weights, targets):
    groups = lax.axis_size(SECTION)
    members = lax.axis_size(TP)
    group = lax.axis_index(SECTION)
    sections, row_count, columns = weights.shape
    micro_tokens = inputs.shape[2]
    all_tokens = inputs.shape[0] * inputs.shape[1] * micro_tokens
    tokens = all_tokens // groups
    per = members // groups
    block = (tokens, columns)
    own_x = lax.dynamic_slice_in_dim(inputs.reshape(all_tokens, columns), group * tokens, tokens, 0)
    own_target = lax.dynamic_slice_in_dim(
        targets.reshape(all_tokens, columns), group * tokens, tokens, 0
    )
    own_x, own_target = lax.optimization_barrier((own_x, own_target))
    blocks, early, late = fetched_matrices(weights, own_x, members)

    scratch = [
        pltpu.VMEM((members * columns, columns), BF16),
        pltpu.SemaphoreType.DMA((ACROSS * CORES,)),
    ]
    early_there, late_there = [
        pltpu.with_memory_space_constraint(array, pltpu.HBM) for array in (early, late)
    ]
    early, late = close(early), close(late)
    kept = []
    x = own_x
    for s in range(sections):
        fetching = s in FETCHING
        if s < EARLY:
            matrices, at = early_there if fetching else early, s
        else:
            matrices, at = late_there if fetching else late, s - EARLY
        outs = [((members,) + block, BF16)] if s < sections - 1 else []
        outs += [(block, BF16), ((2,) + block, F32)]
        kernel = functools.partial(forward_kernel, at, per, fetching)
        given = (kernel, outs, blocks, x, matrices)
        *sent, x, factors = local_call(
            *given, fetching=fetching, scratch=scratch if fetching else ()
        )
        kept.append((blocks, factors))
        if sent:
            blocks = exchanged(sent[0], TP)

    grads_h = []
    received, cotangent = x, own_target
    for s in range(sections - 1, 0, -1):
        matrices, at = (early, s) if s < EARLY else (late, s - EARLY)
        blocks, factors = kept[s]
        outs = [((members,) + block, BF16), (block, BF16), (block, F32)]
        kernel = functools.partial(backward_kernel, at, per, micro_tokens)
        parts, h, cotangent = local_call(
            kernel, outs, received, cotangent, factors, blocks, matrices
        )
        grads_h.insert(0, h)
        received = exchanged(parts, TP)
    (packed,) = local_call(
        functools.partial(last_kernel, per),
        [((groups, sections * (per + 1) * tokens, columns), BF16)],
        received,
        cotangent,
        kept[0][1],
        *[entry[0] for entry in kept],
        *grads_h,
    )
    (result,) = local_call(
        functools.partial(grads_kernel, per, tokens),
        [(weights.shape, BF16)],
        exchanged(packed, SECTION),
    )
    return result


def solution(mesh):
    devices = mesh.devices.reshape(ACROSS, FAR, CORES, mesh.shape[TP])
    finer = Mesh(devices, SECTION + (TP,))
    matrix = P(None, SECTION, TP)
    placed = (P(None, None, None, TP), matrix, P(None, None, None, TP))
    return jax.shard_map(
        on_device, mesh=finer, in_specs=placed, out_specs=matrix, check_vma=False
    )
```

```python
import functools

import jax
import jax.numpy as jnp
from jax import lax
from jax.experimental import pallas as pl
from jax.experimental.pallas import tpu as pltpu
from jax.sharding import Mesh, PartitionSpec as P

EPSILON = 1e-05
F32 = jnp.float32
BF16 = jnp.bfloat16
TP = "tp"
SECTION = ("x", "far", "core")
ACROSS, FAR, CORES = 4, 2, 2
EARLY = 3
FETCHING = (0, 2, EARLY)


def spread(block, copies):
    return lax.optimization_barrier(jnp.broadcast_to(block[None], (copies,) + block.shape))


def exchanged(blocks, axis):
    return lax.all_to_all(blocks, axis, split_axis=0, concat_axis=0, tiled=True)


def swapped(block, axis):
    return lax.ppermute(block, axis, [(0, 1), (1, 0)])


def gathered(shard, crossed):
    pair = jnp.concatenate([shard, crossed], axis=1)
    return pair, functools.partial(lax.all_gather, axis_name=("x", "core"), axis=1, tiled=True)


def fetched_matrices(weights, own_x, members):
    first = weights[:EARLY]
    crossed = swapped(first, "far")
    pair, gather = gathered(first, crossed)
    pair, own_x, last = lax.optimization_barrier((pair, own_x, weights[EARLY:]))
    early = gather(pair)
    crossed_last = swapped(last, "far")
    blocks = exchanged(spread(own_x, members), TP)
    pair, gather = gathered(last, crossed_last)
    pair, blocks = lax.optimization_barrier((pair, blocks))
    late = gather(pair)
    return blocks, early, late


def block_order(per):
    far = lax.axis_index("far")
    order = []
    for x in range(ACROSS):
        for core in range(CORES):
            for q in range(FAR):
                section = (x * FAR + lax.rem(far + q, FAR)) * CORES + core
                order += [per * section + b for b in range(per)]
    return order


def forward_kernel(layer, per, fetching, got, x, matrices, *refs):
    if fetching:
        *refs, held, arrived = refs
    *sent, x_new, factors = refs
    members, tokens, columns = got.shape
    features = members * columns
    order = block_order(per)
    count = ACROSS * CORES
    rows, blocks = features // count, members // count
    copies = []
    for n in range(ACROSS if fetching else 0):
        part = pl.ds(n * CORES * rows, CORES * rows)
        copies.append(
            pltpu.make_async_copy(matrices.at[layer, part], held.at[part], arrived.at[n])
        )
        copies[n].start()
    squares = jnp.zeros(x.shape, F32)
    for m in range(members):
        squares += jnp.square(got[m].astype(F32))
    mean = jnp.sum(squares, axis=1, keepdims=True) / features
    inverse_rms = lax.rsqrt(mean + EPSILON)
    product = jnp.zeros(x.shape, F32)
    for n in range(count):
        segment = jnp.concatenate([got[m] for m in order[n * blocks : (n + 1) * blocks]], axis=1)
        part = pl.ds(n * rows, rows)
        if fetching and n % CORES == 0:
            copies[n // CORES].wait()
        matrix = held[part] if fetching else matrices[layer, part]
        product += jnp.dot(segment, matrix, preferred_element_type=F32)
    activation = inverse_rms * product
    sigmoid = jax.nn.sigmoid(activation)
    result = (x[...].astype(F32) + activation * sigmoid).astype(BF16)
    x_new[...] = result
    for target in sent:
        target[...] = jnp.broadcast_to(result[None], target.shape)
    factors[0] = inverse_rms * sigmoid * (1.0 + activation * (1.0 - sigmoid))
    factors[1] = product * (inverse_rms * inverse_rms / features)


def backward_kernel(layer, per, micro_tokens, received, cotangent, factors, got, matrices, *outs):
    parts, h_out, cot_out = outs
    members, tokens, columns = got.shape
    if len(received.shape) == 2:
        cot = (received[...].astype(F32) - cotangent[...].astype(F32)) / micro_tokens
    else:
        total = cotangent[...]
        for m in range(members):
            total += received[m].astype(F32)
        cot = total.astype(BF16).astype(F32)
    cot_out[...] = cot
    h = (factors[0] * cot).astype(BF16)
    h_out[...] = h
    share = jnp.sum(h.astype(F32) * factors[1], axis=1, keepdims=True)
    order = block_order(per)
    count = ACROSS * CORES
    rows, blocks = members * columns // count, members // count
    for n in range(count):
        back = lax.dot_general(
            h,
            matrices[layer, pl.ds(n * rows, rows)],
            (((1,), (1,)), ((), ())),
            preferred_element_type=F32,
        )
        for k in range(blocks):
            m = order[n * blocks + k]
            mine = back[:, k * columns : (k + 1) * columns] - share * got[m].astype(F32)
            parts[m] = mine.astype(BF16)


def last_kernel(per, received, cotangent, factors, *refs):
    *others, packed = refs
    sections = (len(others) + 1) // 2
    gots, later = others[:sections], others[sections:]
    tokens = cotangent.shape[0]
    total = cotangent[...]
    for m in range(received.shape[0]):
        total += received[m].astype(F32)
    h = (factors[0] * total.astype(BF16).astype(F32)).astype(BF16)
    for s, block in enumerate([h] + [other[...] for other in later]):
        for g in range(packed.shape[0]):
            at = s * (per + 1) * tokens
            for b in range(per):
                packed[g, pl.ds(at + b * tokens, tokens)] = gots[s][per * g + b]
            packed[g, pl.ds(at + per * tokens, tokens)] = block


def grads_kernel(per, tokens, arrived, out):
    groups, _, columns = arrived.shape
    for s in range(out.shape[0]):
        at = s * (per + 1) * tokens
        gathered = [
            jnp.concatenate(
                [arrived[g, pl.ds(at + b * tokens, tokens)] for g in range(groups)], axis=0
            )
            for b in range(per + 1)
        ]
        for b in range(per):
            total = lax.dot_general(
                gathered[b], gathered[per], (((0,), (0,)), ((), ())), preferred_element_type=F32
            )
            out[s, pl.ds(b * columns, columns)] = total.astype(BF16)


def local_call(kernel, outs, *inputs, fetching=False, scratch=()):
    vmem = pl.BlockSpec(memory_space=pltpu.VMEM)
    there = pl.BlockSpec(memory_space=pl.ANY)
    call = pl.pallas_call(
        kernel,
        out_shape=[jax.ShapeDtypeStruct(shape, dtype) for shape, dtype in outs],
        in_specs=[vmem] * (len(inputs) - fetching) + [there] * fetching,
        out_specs=[vmem] * len(outs),
        scratch_shapes=list(scratch),
        compiler_params=pltpu.CompilerParams(vmem_limit_bytes=32 * 2**20),
    )
    return call(*inputs)


def close(array):
    return pltpu.with_memory_space_constraint(array, pltpu.VMEM)


def on_device(inputs, weights, targets):
    groups = lax.axis_size(SECTION)
    members = lax.axis_size(TP)
    group = lax.axis_index(SECTION)
    sections, row_count, columns = weights.shape
    micro_tokens = inputs.shape[2]
    all_tokens = inputs.shape[0] * inputs.shape[1] * micro_tokens
    tokens = all_tokens // groups
    per = members // groups
    block = (tokens, columns)
    own_x = lax.dynamic_slice_in_dim(inputs.reshape(all_tokens, columns), group * tokens, tokens, 0)
    own_target = lax.dynamic_slice_in_dim(
        targets.reshape(all_tokens, columns), group * tokens, tokens, 0
    )
    own_x, own_target = lax.optimization_barrier((own_x, own_target))
    blocks, early, late = fetched_matrices(weights, own_x, members)

    scratch = [
        pltpu.VMEM((members * columns, columns), BF16),
        pltpu.SemaphoreType.DMA((ACROSS,)),
    ]
    early_there, late_there = [
        pltpu.with_memory_space_constraint(array, pltpu.HBM) for array in (early, late)
    ]
    early, late = close(early), close(late)
    kept = []
    x = own_x
    for s in range(sections):
        fetching = s in FETCHING
        if s < EARLY:
            matrices, at = early_there if fetching else early, s
        else:
            matrices, at = late_there if fetching else late, s - EARLY
        outs = [((members,) + block, BF16)] if s < sections - 1 else []
        outs += [(block, BF16), ((2,) + block, F32)]
        kernel = functools.partial(forward_kernel, at, per, fetching)
        given = (kernel, outs, blocks, x, matrices)
        *sent, x, factors = local_call(
            *given, fetching=fetching, scratch=scratch if fetching else ()
        )
        kept.append((blocks, factors))
        if sent:
            blocks = exchanged(sent[0], TP)

    grads_h = []
    received, cotangent = x, own_target
    for s in range(sections - 1, 0, -1):
        matrices, at = (early, s) if s < EARLY else (late, s - EARLY)
        blocks, factors = kept[s]
        outs = [((members,) + block, BF16), (block, BF16), (block, F32)]
        kernel = functools.partial(backward_kernel, at, per, micro_tokens)
        parts, h, cotangent = local_call(
            kernel, outs, received, cotangent, factors, blocks, matrices
        )
        grads_h.insert(0, h)
        received = exchanged(parts, TP)
    (packed,) = local_call(
        functools.partial(last_kernel, per),
        [((groups, sections * (per + 1) * tokens, columns), BF16)],
        received,
        cotangent,
        kept[0][1],
        *[entry[0] for entry in kept],
        *grads_h,
    )
    (result,) = local_call(
        functools.partial(grads_kernel, per, tokens),
        [(weights.shape, BF16)],
        exchanged(packed, SECTION),
    )
    return result


def solution(mesh):
    devices = mesh.devices.reshape(ACROSS, FAR, CORES, mesh.shape[TP])
    finer = Mesh(devices, SECTION + (TP,))
    matrix = P(None, SECTION, TP)
    placed = (P(None, None, None, TP), matrix, P(None, None, None, TP))
    return jax.shard_map(
        on_device, mesh=finer, in_specs=placed, out_specs=matrix, check_vma=False
    )
```
